32 devices in a mesh: groups: 2 (over y), dp: 4 (over x, core), tensor: 4 (over z).
Axes of the slice: x: 2, y: 2, z: 4, core: 2. Of those that a mesh axis runs over, the one named last changes fastest.
Arguments:
- queries: bfloat16 [64, 8192], P(('groups', 'dp')), parts along dimension 0, may hold values from -16 to 16
- key_cache: bfloat16 [64, 512, 1024], P(('groups', 'dp'), 'tensor'), parts along dimension 0, may hold values from -4.5 to 4.5
- value_cache: bfloat16 [64, 512, 1024], P(('groups', 'dp'), 'tensor'), parts along dimension 0, may hold values from -24 to 24
- new_key: bfloat16 [64, 1024], P(('groups', 'dp')), parts along dimension 0, may hold values from -4.5 to 4.5
- new_value: bfloat16 [64, 1024], P(('groups', 'dp')), parts along dimension 0, may hold values from -24 to 24
- lengths: int32 [64], P(('groups', 'dp')), parts along dimension 0, may hold values from 1 to 512, 8192 in all
- out_weight: bfloat16 [8192, 6144], P('tensor'), may hold values from -0.375 to 0.375
- quant_scale: float32 [6144], replicated, may hold values from 0.0003 to 0.003
- residual: bfloat16 [64, 6144], P(('groups', 'dp')), parts along dimension 0, may hold values from -60 to 60
- norm_gain: bfloat16 [6144], replicated, may hold values from 0.5 to 1.5
Outputs:
- new_residual: bfloat16 [64, 6144], P(('groups', 'dp')), parts along dimension 0
- normed: bfloat16 [64, 6144], P(('groups', 'dp')), parts along dimension 0
The draws below stay inside these ranges and needn't reach their ends.
There are 2 independent parts, one for each index of `groups`. The reference program is written for one: setup_inputs(seed, part) draws one part's arguments, and reference() takes and returns one part's arrays. A program takes and returns all parts, laid end to end along the dimension named above; an argument that names none is the same for every part. Nothing has to cross between parts.
Inputs may be any that keep to these rules, and one draw needn't show every extreme that they name: Row r attends to cache positions 0 to lengths[r] - 1 and to its new key.
All inputs are finite; a program needn't handle non-finite values. No bound on the sum of `lengths` on one device may be relied on, other than what follows from the above.
Results may differ from the reference program's by a relative error of at most 0.0085.
Values may be sent and summed in bfloat16 or wider, within the bound.
No kernel may reach another device: no remote copies, remote signals or barrier semaphores. Data moves between devices by JAX's collectives and lax.ppermute only.
A program may use at most 128 MiB of HBM per device.

```python
import math
import jax
import jax.numpy as jnp
import numpy as np
from jax import lax

L = 512
D = 6144
QH = 64
KVH = 8
HD = 128
HB = 64
HEADS_DEV = 16
ROWS = 32


def first_uniform(key):
    return jax.random.uniform(jax.random.fold_in(key, 102), (ROWS, 1, KVH * HD), jnp.float32, 1e-06, 1.0 - 1e-06)


def later_uniform(key):
    return jax.random.uniform(jax.random.fold_in(key, 101), (ROWS, L - 1, KVH * HD), jnp.float32, 1e-06, 1.0 - 1e-06)


def draw_key_cache(key, part):
    shared = jnp.concatenate([first_uniform(key), later_uniform(key)], axis=1)
    result = jnp.clip(0.5513 * jnp.log(shared / (1.0 - shared)), -4.5, 4.5)
    return result.astype(jnp.bfloat16)


def draw_queries(key, part):
    key = jax.random.fold_in(key, 5)
    group_size = QH // KVH
    result = jnp.clip(jax.random.normal(key, (ROWS, KVH, group_size, HD), jnp.float32), -4.0, 4.0)
    return result.reshape(ROWS, QH * HD).astype(jnp.bfloat16)


def draw_new_key(key, part):
    key = jax.random.fold_in(key, 7)
    result = jnp.clip(jax.random.normal(key, (ROWS, KVH * HD), jnp.float32), -4.5, 4.5)
    return result.astype(jnp.bfloat16)


def draw_residual(key, part):
    key = jax.random.fold_in(key, 11)
    key_base, key_rows = jax.random.split(key, 2)
    column_scale = 0.25 * 10.0 ** (jnp.arange(D, dtype=jnp.float32) / D)
    row_scale = jnp.exp(jax.random.uniform(key_rows, (ROWS, 1), jnp.float32, 0.0, math.log(4.0)))
    base_draw = jnp.clip(jax.random.normal(key_base, (ROWS, D), jnp.float32), -6.0, 6.0)
    return (base_draw * column_scale[None, :] * row_scale).astype(jnp.bfloat16)


def spiked(values, own_key, source, target, blocks, factor):
    def block_of(position):
        return (jnp.arange(values.shape[position]) // (values.shape[position] // blocks)).reshape((-1,) + (1,) * (values.ndim - 1 - position))

    first = jax.random.permutation(own_key, blocks)[block_of(target)]
    second = (block_of(target) + blocks // 2) % blocks
    return jnp.where((block_of(source) == first) | (block_of(source) == second), factor * values, values)


def block_levels(own_key, shape, cuts, least, high):
    factor_of = 1.0
    for position, parts in cuts:
        draws = jax.random.uniform(jax.random.fold_in(jax.random.fold_in(own_key, 6), position), (parts,), jnp.float32, least / len(cuts), high / len(cuts))
        factor_of = factor_of * jnp.repeat(jnp.exp(draws), shape[position] // parts).reshape((-1,) + (1,) * (len(shape) - 1 - position))
    return factor_of


def split_up(count, total, bound, slope):
    weights = [(1 << 20) // math.isqrt(standing ** slope) + 1 for standing in range(2, count + 1)]
    rest, given = total - bound - (count - 1), [1] * (count - 1)
    while rest > 0:
        free = [i for i in range(count - 1) if given[i] < bound]
        whole, remaining = sum([weights[i] for i in free]), rest
        for i in free:
            addition = min(bound - given[i], max(1, remaining * weights[i] // whole), rest)
            given[i] = given[i] + addition
            rest = rest - addition
    return np.array([bound] + given)


def ragged(own_key, count, total, limit, slope):
    if count == 2:
        one = jax.random.randint(own_key, (), max(1, total - limit), min(limit, total - 1) + 1)
        return jnp.stack([one, total - one])
    sizes = jnp.asarray(split_up(count, total, limit, slope), jnp.int32)
    twos = (count - 1) // 2
    source_of, taker = sizes[1:1 + 2 * twos:2], sizes[2:2 + 2 * twos:2]
    room = jnp.minimum(source_of - 1, limit - taker)
    moved = jax.random.randint(jax.random.fold_in(own_key, 1), (twos,), 0, 1 << 20) % (room + 1)
    sizes = sizes.at[1:1 + 2 * twos:2].set(source_of - moved).at[2:2 + 2 * twos:2].set(taker + moved)
    return sizes[jax.random.permutation(jax.random.fold_in(own_key, 2), count)]


def scatter_about(stream_key, dims, width, most, shards=(), held_as=jnp.bfloat16):
    values = width * jax.random.normal(stream_key, dims, jnp.float32)
    if shards:
        values = values * block_levels(stream_key, dims, shards, -0.22, 0.18)
    return jnp.clip(values, -most, most).astype(held_as)


def heavy_noise(own_key, shape, width, reach, cuts, heavy, kind=jnp.bfloat16):
    array = width * jax.random.normal(own_key, shape, jnp.float32)
    if cuts:
        array = array * block_levels(own_key, shape, cuts, -0.22, 0.18)
    return jnp.clip(spiked(array, jax.random.fold_in(own_key, 3), *heavy), -reach, reach).astype(kind)


def setup_inputs(seed: int = 0, part: int = 0) -> dict:
    key_of = jax.random.split(jax.random.key(seed), 11)
    own_keys = jax.random.split(jax.random.fold_in(key_of[10], part), 11)
    queries = draw_queries(jax.random.fold_in(jax.random.fold_in(key_of[10], part), 71), part)
    key_cache = draw_key_cache(jax.random.fold_in(jax.random.fold_in(key_of[10], part), 71), part)
    value_cache = scatter_about(own_keys[2], (ROWS, L, KVH * HD), 4.0, 24.0, ((0, 4), (1, 4)))
    new_key = draw_new_key(jax.random.fold_in(jax.random.fold_in(key_of[10], part), 71), part)
    new_value = scatter_about(own_keys[4], (ROWS, KVH * HD), 4.0, 24.0, ((0, 4),))
    lengths = ragged(own_keys[5], ROWS, ROWS * L // 2, L, 2).astype(jnp.int32)
    out_weight = heavy_noise(key_of[6], (QH * HD, D), (QH * HD // 16) ** -0.5, 0.375, ((0, 4),), (0, 1, 4, 2.0))
    quant_scale = jnp.clip(jnp.exp(jax.random.uniform(key_of[7], (D,), jnp.float32, math.log(0.0003), math.log(0.003))), 0.0003, 0.003)
    residual = draw_residual(jax.random.fold_in(jax.random.fold_in(key_of[10], part), 71), part)
    norm_gain = jnp.clip(1.0 + 0.1 * jax.random.normal(key_of[9], (D,), jnp.float32), 0.5, 1.5).astype(jnp.bfloat16)
    return dict(queries=queries, key_cache=key_cache, value_cache=value_cache, new_key=new_key, new_value=new_value, lengths=lengths, out_weight=out_weight, quant_scale=quant_scale, residual=residual, norm_gain=norm_gain)


neg_fill = -1e+30
fp8_most = 448.0
norm_eps = 1e-05

def hadamard_matrix(block_size):
    indices = jnp.arange(block_size, dtype=jnp.int32)
    intersection = jnp.bitwise_and(indices[:, None], indices[None, :])
    parity = jnp.zeros((block_size, block_size), jnp.int32)
    for bit_index in range(max(block_size.bit_length() - 1, 1)):
        parity = parity + jnp.bitwise_and(jnp.right_shift(intersection, bit_index), 1)
    sign_table = 1.0 - 2.0 * jnp.bitwise_and(parity, 1).astype(jnp.float32)
    return sign_table / math.sqrt(block_size)

def rotate_blocks(values, hadamard):
    block_size = hadamard.shape[0]
    full_shape = values.shape
    blocked = values.reshape(full_shape[:-1] + (full_shape[-1] // block_size, block_size))
    turned = jnp.einsum('rbi,ij->rbj', blocked, hadamard, precision=lax.Precision.HIGHEST)
    return turned.reshape(full_shape)

def attend_row(packed):
    query_row, key_rows, value_rows, self_key, self_value, length = packed
    group_size = QH // KVH
    score_scale = 1.0 / math.sqrt(HD)
    query_heads = query_row.reshape(KVH, group_size, HD).astype(jnp.float32)
    cache_scores = jnp.einsum('kgd,pkd->kgp', query_heads, key_rows.reshape(L, KVH, HD).astype(jnp.float32)) * score_scale
    valid_mask = jnp.arange(L, dtype=jnp.int32) < length
    cache_scores = jnp.where(valid_mask[None, None, :], cache_scores, neg_fill)
    self_score = jnp.einsum('kgd,kd->kg', query_heads, self_key.reshape(KVH, HD).astype(jnp.float32)) * score_scale
    row_top = jnp.maximum(lax.optimization_barrier(jnp.max(cache_scores, axis=-1)), self_score)
    cache_weights = jnp.where(valid_mask[None, None, :], jnp.exp(cache_scores - row_top[..., None]), 0.0)
    self_weight = jnp.exp(self_score - row_top)
    weight_sum = lax.optimization_barrier(jnp.sum(cache_weights, axis=-1)) + self_weight
    rounded_cache = lax.optimization_barrier(cache_weights.astype(jnp.bfloat16)).astype(jnp.float32)
    rounded_self = lax.optimization_barrier(self_weight.astype(jnp.bfloat16)).astype(jnp.float32)
    weighted = jnp.einsum('kgp,pkd->kgd', rounded_cache, value_rows.reshape(L, KVH, HD).astype(jnp.float32))
    weighted = weighted + rounded_self[..., None] * self_value.reshape(KVH, 1, HD).astype(jnp.float32)
    return (weighted / weight_sum[..., None]).astype(jnp.bfloat16).reshape(QH * HD)

def reference(queries, key_cache, value_cache, new_key, new_value, lengths, out_weight, quant_scale, residual, norm_gain):
    attention = lax.map(attend_row, (queries, key_cache, value_cache, new_key, new_value, lengths))
    hadamard = hadamard_matrix(HB)
    width_dev = HEADS_DEV * HD

    def add_partial(running, part_index):
        col_start = (part_index * width_dev).astype(jnp.int32)
        attn_piece = lax.dynamic_slice_in_dim(attention, col_start, width_dev, 1)
        weight_rows = lax.dynamic_slice_in_dim(out_weight, col_start, width_dev, 0)
        partial_out = jnp.dot(attn_piece, weight_rows, preferred_element_type=jnp.float32)
        rotated = rotate_blocks(partial_out, hadamard)
        coded_out = jnp.clip(rotated / quant_scale, -fp8_most, fp8_most).astype(jnp.bfloat16)
        return (running + lax.optimization_barrier(coded_out).astype(jnp.float32), None)
    summed, unused = lax.scan(add_partial, jnp.zeros((ROWS, D), jnp.float32), jnp.arange(QH // HEADS_DEV, dtype=jnp.int32))
    restored = rotate_blocks(summed * quant_scale, hadamard)
    combined = residual.astype(jnp.float32) + restored
    new_residual = combined.astype(jnp.bfloat16)
    mean_square = lax.optimization_barrier(jnp.mean(combined * combined, axis=-1, keepdims=True))
    normed = (combined * lax.rsqrt(mean_square + norm_eps) * norm_gain.astype(jnp.float32)).astype(jnp.bfloat16)
    return (new_residual, normed)
```

```python
import functools
import math

import jax
import jax.numpy as jnp
import numpy as np
from jax import lax
from jax.experimental import pallas as pl
from jax.experimental.pallas import tpu as pltpu
from jax.sharding import PartitionSpec as P

QH = 64
KVH = 8
HD = 128
HB = 64
GROUP = QH // KVH
TURN = 256
STATS = 16

neg_fill = -1e30
coded_most = 448.0
norm_eps = 1e-05


def hadamard_tile():
    index = np.arange(TURN)
    both = (index[:, None] % HB) & (index[None, :] % HB)
    parity = np.zeros((TURN, TURN), np.int64)
    for bit in range(HB.bit_length() - 1):
        parity += (both >> bit) & 1
    signs = 1.0 - 2.0 * (parity % 2)
    same = (index[:, None] // HB) == (index[None, :] // HB)
    return np.where(same, signs, 0.0) / math.sqrt(HB)


def rotate(values, hadamard):
    rows, width = values.shape
    stacked = jnp.concatenate(
        [values[:, at : at + TURN] for at in range(0, width, TURN)], axis=0
    )
    high = stacked.astype(jnp.bfloat16)
    low = (stacked - high.astype(jnp.float32)).astype(jnp.bfloat16)
    turned = jnp.dot(high, hadamard, preferred_element_type=jnp.float32) + jnp.dot(
        low, hadamard, preferred_element_type=jnp.float32
    )
    return jnp.concatenate(
        [turned[at : at + rows] for at in range(0, turned.shape[0], rows)], axis=1
    )


def attend_kernel(
    parts, lengths, queries, new_key, new_value, key_hbm, value_hbm, *refs
):
    outs = refs[:parts]
    keys, values, q_rows, o_rows, top_rows, sum_rows, sems = refs[parts:]
    row_count, places, _ = keys.shape
    chunk = QH // parts * row_count
    me = lax.axis_index("tensor")
    first = me == 0
    scale = 1.0 / math.sqrt(HD)

    copies = []
    for r in range(row_count):
        pair = (
            pltpu.make_async_copy(key_hbm.at[r], keys.at[r], sems.at[0, r]),
            pltpu.make_async_copy(value_hbm.at[r], values.at[r], sems.at[1, r]),
        )
        pair[0].start()
        pair[1].start()
        copies.append(pair)

    for h in range(QH):
        q_rows[h * row_count : (h + 1) * row_count, :] = queries[
            :, h * HD : (h + 1) * HD
        ].astype(jnp.float32)
    self_keys = new_key[...].astype(jnp.float32)
    self_values = new_value[...].astype(jnp.float32)

    def by_head(row):
        return jnp.concatenate(
            [
                jnp.broadcast_to(row[:, k * HD : (k + 1) * HD], (GROUP, HD))
                for k in range(KVH)
            ],
            axis=0,
        )

    upper = lax.broadcasted_iota(jnp.int32, (2 * GROUP, HD), 0) < GROUP
    position = me * places + lax.broadcasted_iota(jnp.int32, (QH, places), 1)
    for r in range(row_count):
        q_r = q_rows[pl.ds(r, QH, stride=row_count), :]
        self_score = (
            jnp.sum(q_r * by_head(self_keys[r : r + 1]), axis=1, keepdims=True) * scale
        )
        self_score = jnp.where(first, self_score, neg_fill)
        copies[r][0].wait()
        scores = []
        for t in range(KVH // 2):
            two = q_r[2 * GROUP * t : 2 * GROUP * (t + 1)]
            two = jnp.concatenate(
                [jnp.where(upper, two, 0.0), jnp.where(upper, 0.0, two)], axis=1
            ).astype(jnp.bfloat16)
            scores.append(
                lax.dot_general(
                    two,
                    keys[r, :, 2 * HD * t : 2 * HD * (t + 1)],
                    (((1,), (1,)), ((), ())),
                    preferred_element_type=jnp.float32,
                )
            )
        scores = jnp.concatenate(scores, axis=0) * scale
        valid = position < lengths[r]
        scores = jnp.where(valid, scores, neg_fill)
        top = jnp.maximum(jnp.max(scores, axis=1, keepdims=True), self_score)
        weights = jnp.where(valid, jnp.exp(scores - top), 0.0)
        self_weight = jnp.where(first, jnp.exp(self_score - top), 0.0)
        total = jnp.sum(weights, axis=1, keepdims=True) + self_weight
        rounded = weights.astype(jnp.bfloat16)
        copies[r][1].wait()
        pieces = []
        for t in range(KVH // 2):
            both = jnp.dot(
                rounded[2 * GROUP * t : 2 * GROUP * (t + 1)],
                values[r, :, 2 * HD * t : 2 * HD * (t + 1)],
                preferred_element_type=jnp.float32,
            )
            pieces.append(both[:GROUP, :HD])
            pieces.append(both[GROUP:, HD:])
        rounded_self = self_weight.astype(jnp.bfloat16).astype(jnp.float32)
        weighted = jnp.concatenate(pieces, axis=0) + rounded_self * by_head(
            self_values[r : r + 1]
        )
        at = pl.ds(r, QH, stride=row_count)
        o_rows[at, :] = weighted
        top_rows[at, :] = jnp.broadcast_to(top, (QH, HD))
        sum_rows[at, :] = jnp.broadcast_to(total, (QH, HD))

    eye = lax.broadcasted_iota(jnp.int32, (chunk, HD), 0) == lax.broadcasted_iota(
        jnp.int32, (chunk, HD), 1
    )

    def terms(rows):
        lane = jnp.sum(jnp.where(eye, rows, 0.0), axis=0, keepdims=True)
        found = []
        for _ in range(3):
            high = lane.astype(jnp.bfloat16).astype(jnp.float32)
            found.append(high)
            lane = lane - high
        return found

    for s in range(parts):
        to = lax.rem(me + s, parts)
        block = pl.ds(pl.multiple_of(to * chunk, chunk), chunk)
        outs[s][:chunk, :] = o_rows[block, :].astype(jnp.bfloat16)
        lines = terms(top_rows[block, :]) + terms(sum_rows[block, :])
        lines.append(jnp.zeros((STATS - len(lines), HD), jnp.float32))
        outs[s][chunk:, :] = jnp.concatenate(lines, axis=0).astype(jnp.bfloat16)


def project_kernel(parts, *refs):
    messages = refs[:parts]
    weight, quant_scale, hadamard, coded = refs[parts:]
    row_count = coded.shape[0]
    chunk = messages[0].shape[0] - STATS
    tops, sums = [], []
    for message in messages:
        lines = message[chunk:, :].astype(jnp.float32)
        tops.append(lines[0:1] + lines[1:2] + lines[2:3])
        sums.append(lines[3:4] + lines[4:5] + lines[5:6])
    top = functools.reduce(jnp.maximum, tops)
    factors = [jnp.exp(one - top) for one in tops]
    total = functools.reduce(jnp.add, [f * one for f, one in zip(factors, sums)])
    shares = [f / total for f in factors]
    padded = -len(shares) % 8
    shares = jnp.concatenate(
        shares + [jnp.zeros((padded, HD), jnp.float32)] * (padded > 0), axis=0
    )
    shares = shares.T
    mixed = functools.reduce(
        jnp.add,
        [
            message[:chunk, :].astype(jnp.float32) * shares[:chunk, s : s + 1]
            for s, message in enumerate(messages)
        ],
    )
    attention = jnp.concatenate(
        [mixed[at : at + row_count] for at in range(0, chunk, row_count)], axis=1
    ).astype(jnp.bfloat16)
    width = coded.shape[1]
    step = 512
    for at in range(0, width, step):
        out = jnp.dot(
            attention, weight[:, at : at + step], preferred_element_type=jnp.float32
        )
        turned = rotate(out, hadamard[...])
        coded[:, at : at + step] = jnp.clip(
            turned / quant_scale[:, at : at + step], -coded_most, coded_most
        ).astype(jnp.bfloat16)


def finish_kernel(
    mine, theirs, quant_scale, hadamard, residual, gain, new_residual, normed
):
    summed = mine[...].astype(jnp.float32) + theirs[...].astype(jnp.float32)
    restored = rotate(summed * quant_scale[...], hadamard[...])
    combined = residual[...].astype(jnp.float32) + restored
    mean_square = jnp.mean(combined * combined, axis=1, keepdims=True)
    new_residual[...] = combined.astype(jnp.bfloat16)
    normed[...] = (
        combined * lax.rsqrt(mean_square + norm_eps) * gain[...].astype(jnp.float32)
    ).astype(jnp.bfloat16)


VM = pl.BlockSpec(memory_space=pltpu.VMEM)
SM = pl.BlockSpec(memory_space=pltpu.SMEM)
ANY = pl.BlockSpec(memory_space=pl.ANY)
MIB = 1 << 20


def body(
    queries,
    key_cache,
    value_cache,
    new_key,
    new_value,
    lengths,
    out_weight,
    quant_scale,
    residual,
    norm_gain,
):
    row_count, places, kv_width = key_cache.shape
    parts = lax.axis_size("tensor")
    width = out_weight.shape[1]
    chunk = QH // parts * row_count
    hadamard = jnp.asarray(hadamard_tile(), jnp.bfloat16)
    scale_row = quant_scale.reshape(1, width)
    gain_row = norm_gain.reshape(1, width)

    with jax.named_scope("attend"):
        messages = pl.pallas_call(
            functools.partial(attend_kernel, parts),
            out_shape=[
                jax.ShapeDtypeStruct((chunk + STATS, HD), jnp.bfloat16)
                for _ in range(parts)
            ],
            in_specs=[SM, VM, VM, VM, ANY, ANY],
            out_specs=[VM] * parts,
            scratch_shapes=[
                pltpu.VMEM((row_count, places, kv_width), jnp.bfloat16),
                pltpu.VMEM((row_count, places, kv_width), jnp.bfloat16),
                pltpu.VMEM((QH * row_count, HD), jnp.float32),
                pltpu.VMEM((QH * row_count, HD), jnp.float32),
                pltpu.VMEM((QH * row_count, HD), jnp.float32),
                pltpu.VMEM((QH * row_count, HD), jnp.float32),
                pltpu.SemaphoreType.DMA((2, row_count)),
            ],
            compiler_params=pltpu.CompilerParams(vmem_limit_bytes=16 * MIB),
        )(lengths, queries, new_key, new_value, key_cache, value_cache)

    with jax.named_scope("exchange"):
        gathered = [messages[0]]
        for s in range(1, parts):
            gathered.append(
                lax.ppermute(
                    messages[s], "tensor", [(i, (i + s) % parts) for i in range(parts)]
                )
            )

    with jax.named_scope("project"):
        weight = pltpu.with_memory_space_constraint(out_weight, pltpu.VMEM)
        coded = pl.pallas_call(
            functools.partial(project_kernel, parts),
            out_shape=jax.ShapeDtypeStruct((row_count, width), jnp.bfloat16),
            in_specs=[VM] * (parts + 3),
            out_specs=VM,
            compiler_params=pltpu.CompilerParams(vmem_limit_bytes=16 * MIB),
        )(*gathered, weight, scale_row, hadamard)

    with jax.named_scope("reduce"):
        held = coded
        stride = 1
        while stride < parts:
            arrived = lax.ppermute(
                held, "tensor", [(i, i ^ stride) for i in range(parts)]
            )
            stride *= 2
            if stride < parts:
                held = (held.astype(jnp.float32) + arrived.astype(jnp.float32)).astype(
                    jnp.bfloat16
                )

    with jax.named_scope("finish"):
        return pl.pallas_call(
            finish_kernel,
            out_shape=[jax.ShapeDtypeStruct((row_count, width), jnp.bfloat16)] * 2,
            in_specs=[VM] * 6,
            out_specs=[VM] * 2,
            compiler_params=pltpu.CompilerParams(vmem_limit_bytes=16 * MIB),
        )(held, arrived, scale_row, hadamard, residual, gain_row)


def solution(mesh):
    placed = (
        P(("groups", "dp"), None),
        P(("groups", "dp"), "tensor", None),
        P(("groups", "dp"), "tensor", None),
        P(("groups", "dp"), None),
        P(("groups", "dp"), None),
        P(("groups", "dp")),
        P("tensor", None),
        P(),
        P(("groups", "dp"), None),
        P(),
    )
    return jax.shard_map(
        body,
        mesh=mesh,
        in_specs=placed,
        out_specs=(P(("groups", "dp"), None), P(("groups", "dp"), None)),
        check_vma=False,
    )
```

```python
import functools
import math

import jax
import jax.numpy as jnp
import numpy as np
from jax import lax
from jax.experimental import pallas as pl
from jax.experimental.pallas import tpu as pltpu
from jax.sharding import PartitionSpec as P

QH = 64
KVH = 8
HD = 128
HB = 64
GROUP = QH // KVH
TURN = 256
TERMS = 3
STATS = 32
EXTRA = 16

neg_fill = -1e30
coded_most = 448.0
norm_eps = 1e-05

EARLY = 1024
MIDDLE = 2560
PIECE = 512


def hadamard_tile():
    index = np.arange(TURN)
    both = (index[:, None] % HB) & (index[None, :] % HB)
    parity = np.zeros((TURN, TURN), np.int64)
    for bit in range(HB.bit_length() - 1):
        parity += (both >> bit) & 1
    signs = 1.0 - 2.0 * (parity % 2)
    same = (index[:, None] // HB) == (index[None, :] // HB)
    return np.where(same, signs, 0.0) / math.sqrt(HB)


def rotate(values, hadamard):
    rows, width = values.shape
    stacked = jnp.concatenate(
        [values[:, at : at + TURN] for at in range(0, width, TURN)], axis=0
    )
    high = stacked.astype(jnp.bfloat16)
    low = (stacked - high.astype(jnp.float32)).astype(jnp.bfloat16)
    turned = jnp.dot(high, hadamard, preferred_element_type=jnp.float32) + jnp.dot(
        low, hadamard, preferred_element_type=jnp.float32
    )
    return jnp.concatenate(
        [turned[at : at + rows] for at in range(0, turned.shape[0], rows)], axis=1
    )


def column_copies(source, target, sems, start):
    copies = []
    for k in range(target.shape[1] // PIECE):
        copies.append(
            pltpu.make_async_copy(
                source.at[:, pl.ds(start + k * PIECE, PIECE)],
                target.at[:, pl.ds(k * PIECE, PIECE)],
                sems.at[k],
            )
        )
    return copies


def attend_kernel(
    parts,
    lengths,
    queries_hbm,
    new_key_hbm,
    new_value_hbm,
    key_hbm,
    value_hbm,
    weight_hbm,
    *refs,
):
    outs = refs[:parts]
    early = refs[parts]
    (
        queries,
        new_key,
        new_value,
        keys,
        values,
        q_rows,
        o_rows,
        small_sems,
        sems,
        early_sems,
    ) = refs[parts + 1 :]
    row_count, places, _ = key_hbm.shape
    half = row_count // 2
    chunk = QH // parts * row_count
    me = lax.axis_index("tensor")
    scale = 1.0 / math.sqrt(HD)

    small = [
        pltpu.make_async_copy(queries_hbm, queries, small_sems.at[0]),
        pltpu.make_async_copy(new_key_hbm, new_key, small_sems.at[1]),
        pltpu.make_async_copy(new_value_hbm, new_value, small_sems.at[2]),
    ]
    for copy in small:
        copy.start()
    pairs = [(p, p + half) for p in range(half)]
    cached = pl.ds(0, places)
    key_copies = {}
    value_copies = {}
    for pair in pairs:
        for r in pair:
            key_copies[r] = pltpu.make_async_copy(
                key_hbm.at[r], keys.at[r, cached], sems.at[0, r]
            )
            key_copies[r].start()
    for pair in pairs:
        for r in pair:
            value_copies[r] = pltpu.make_async_copy(
                value_hbm.at[r], values.at[r, cached], sems.at[1, r]
            )
            value_copies[r].start()
    ahead = column_copies(weight_hbm, early, early_sems, 0)
    for copy in ahead:
        copy.start()

    for copy in small:
        copy.wait()
    for h in range(QH):
        q_rows[h * row_count : (h + 1) * row_count, :] = queries[
            :, h * HD : (h + 1) * HD
        ].astype(jnp.float32)
    extra = pl.ds(places, EXTRA)
    for r in range(row_count):
        wide = (EXTRA, KVH * HD)
        keys[r, extra, :] = jnp.broadcast_to(new_key[r : r + 1, :], wide)
        values[r, extra, :] = jnp.broadcast_to(new_value[r : r + 1, :], wide)

    lane = lax.broadcasted_iota(jnp.int32, (HD, 2 * QH), 1)
    place = lax.broadcasted_iota(jnp.int32, (places + EXTRA, 2 * QH), 0)
    lane_side = lax.broadcasted_iota(jnp.int32, (places + EXTRA, 2 * QH), 1) < QH
    place_end = jnp.where(me == 0, places + 1, places)
    scores = []
    for pair in pairs:
        both = jnp.concatenate(
            [q_rows[pl.ds(r, QH, stride=row_count), :] for r in pair], axis=0
        )
        turned = both.T
        score = 0.0
        for e, r in enumerate(pair):
            key_copies[r].wait()
            spread = jnp.concatenate(
                [
                    jnp.where(lane // GROUP == e * KVH + k, turned, 0.0)
                    for k in range(KVH)
                ],
                axis=0,
            ).astype(jnp.bfloat16)
            score = score + jnp.dot(
                keys[r], spread, preferred_element_type=jnp.float32
            )
        scores.append(score * scale)
    tops, sums, weights = [], [], []
    for pair, score in zip(pairs, scores):
        limit = [jnp.minimum(lengths[r] - me * places, places) for r in pair]
        valid = (place < jnp.where(lane_side, limit[0], limit[1])) | (
            (place >= places) & (place < place_end)
        )
        score = jnp.where(valid, score, neg_fill)
        top = jnp.max(score, axis=0, keepdims=True)
        weight = jnp.where(valid, jnp.exp(score - top), 0.0)
        tops.append(top)
        sums.append(jnp.sum(weight, axis=0, keepdims=True))
        weights.append(weight.T.astype(jnp.bfloat16))
    for pair, weight in zip(pairs, weights):
        for e, r in enumerate(pair):
            value_copies[r].wait()
            pieces = []
            for t in range(KVH // 2):
                at = e * QH + 2 * GROUP * t
                two = jnp.dot(
                    weight[at : at + 2 * GROUP],
                    values[r, :, 2 * HD * t : 2 * HD * (t + 1)],
                    preferred_element_type=jnp.float32,
                )
                pieces.append(two[:GROUP, :HD])
                pieces.append(two[GROUP:, HD:])
            o_rows[pl.ds(r, QH, stride=row_count), :] = jnp.concatenate(pieces, axis=0)

    def by_row(lines):
        lines = jnp.concatenate(lines, axis=0)
        return jnp.concatenate([lines[:, :QH], lines[:, QH:]], axis=0)

    rest = jnp.concatenate([by_row(tops), by_row(sums)], axis=1)
    terms = []
    for _ in range(TERMS):
        high = rest.astype(jnp.bfloat16).astype(jnp.float32)
        terms.append(high)
        rest = rest - high
    terms.append(jnp.zeros((STATS - TERMS * row_count, HD), jnp.float32))
    stats = jnp.concatenate(terms, axis=0).astype(jnp.bfloat16)
    for s in range(parts):
        to = lax.rem(me + s, parts)
        block = pl.ds(pl.multiple_of(to * chunk, chunk), chunk)
        outs[s][:chunk, :] = o_rows[block, :].astype(jnp.bfloat16)
        outs[s][chunk:, :] = stats
    for copy in ahead:
        copy.wait()


def load_kernel(weight_hbm, middle, sems):
    copies = column_copies(weight_hbm, middle, sems, EARLY)
    for copy in copies:
        copy.start()
    for copy in copies:
        copy.wait()


def project_kernel(parts, *refs):
    messages = refs[:parts]
    (
        early,
        middle,
        weight_hbm,
        quant_scale,
        hadamard,
        coded,
        late,
        product,
        sems,
    ) = refs[parts:]
    row_count = coded.shape[0]
    chunk = messages[0].shape[0] - STATS
    heads = chunk // row_count
    me = lax.axis_index("tensor")
    copies = column_copies(weight_hbm, late, sems, EARLY + MIDDLE)
    for copy in copies:
        copy.start()

    tops, sums = [], []
    for message in messages:
        lines = message[chunk:, :].astype(jnp.float32)
        lines = sum(lines[t * row_count : (t + 1) * row_count] for t in range(TERMS))
        tops.append(lines)
        sums.append(pltpu.roll(lines, QH, 1))
    top = functools.reduce(jnp.maximum, tops)
    factors = [jnp.exp(one - top) for one in tops]
    total = functools.reduce(jnp.add, [f * one for f, one in zip(factors, sums)])
    shares = [
        pltpu.roll(f / total, lax.rem(2 * QH - me * heads, 2 * QH), 1) for f in factors
    ]
    mixed = []
    for h in range(heads):
        at = slice(h * row_count, (h + 1) * row_count)
        mixed.append(
            functools.reduce(
                jnp.add,
                [
                    message[at, :].astype(jnp.float32) * share[:, h : h + 1]
                    for share, message in zip(shares, messages)
                ],
            )
        )
    attention = jnp.concatenate(mixed, axis=1).astype(jnp.bfloat16)

    def multiply(held, start, at):
        product[:, start + at : start + at + PIECE] = jnp.dot(
            attention, held[:, at : at + PIECE], preferred_element_type=jnp.float32
        )

    for at in range(0, EARLY, PIECE):
        multiply(early, 0, at)
    for at in range(0, MIDDLE, PIECE):
        multiply(middle, EARLY, at)
    for k, copy in enumerate(copies):
        copy.wait()
        multiply(late, EARLY + MIDDLE, k * PIECE)
    turned = rotate(product[...], hadamard[...])
    coded[...] = jnp.clip(turned / quant_scale[...], -coded_most, coded_most).astype(
        jnp.bfloat16
    )


def finish_kernel(
    mine, theirs, quant_scale, hadamard, residual, gain, new_residual, normed
):
    summed = mine[...].astype(jnp.float32) + theirs[...].astype(jnp.float32)
    restored = rotate(summed * quant_scale[...], hadamard[...])
    combined = residual[...].astype(jnp.float32) + restored
    mean_square = jnp.mean(combined * combined, axis=1, keepdims=True)
    new_residual[...] = combined.astype(jnp.bfloat16)
    normed[...] = (
        combined * lax.rsqrt(mean_square + norm_eps) * gain[...].astype(jnp.float32)
    ).astype(jnp.bfloat16)


VM = pl.BlockSpec(memory_space=pltpu.VMEM)
SM = pl.BlockSpec(memory_space=pltpu.SMEM)
ANY = pl.BlockSpec(memory_space=pl.ANY)
MIB = 1 << 20


def in_hbm(array):
    return pltpu.with_memory_space_constraint(array, pltpu.HBM)


def body(
    queries,
    key_cache,
    value_cache,
    new_key,
    new_value,
    lengths,
    out_weight,
    quant_scale,
    residual,
    norm_gain,
):
    row_count, places, kv_width = key_cache.shape
    parts = lax.axis_size("tensor")
    depth, width = out_weight.shape
    late = width - EARLY - MIDDLE
    chunk = QH // parts * row_count
    hadamard = jnp.asarray(hadamard_tile(), jnp.bfloat16)
    scale_row = quant_scale.reshape(1, width)
    gain_row = norm_gain.reshape(1, width)
    bf16 = jnp.bfloat16

    with jax.named_scope("attend"):
        *messages, early = pl.pallas_call(
            functools.partial(attend_kernel, parts),
            out_shape=[
                jax.ShapeDtypeStruct((chunk + STATS, HD), bf16) for _ in range(parts)
            ]
            + [pltpu.VMEM((depth, EARLY), bf16)],
            in_specs=[SM] + [ANY] * 6,
            out_specs=[VM] * (parts + 1),
            scratch_shapes=[
                pltpu.VMEM(queries.shape, bf16),
                pltpu.VMEM(new_key.shape, bf16),
                pltpu.VMEM(new_value.shape, bf16),
                pltpu.VMEM((row_count, places + EXTRA, kv_width), bf16),
                pltpu.VMEM((row_count, places + EXTRA, kv_width), bf16),
                pltpu.VMEM((QH * row_count, HD), jnp.float32),
                pltpu.VMEM((QH * row_count, HD), jnp.float32),
                pltpu.SemaphoreType.DMA((3,)),
                pltpu.SemaphoreType.DMA((2, row_count)),
                pltpu.SemaphoreType.DMA((EARLY // PIECE,)),
            ],
            compiler_params=pltpu.CompilerParams(vmem_limit_bytes=12 * MIB),
        )(
            lengths,
            *[
                in_hbm(array)
                for array in (
                    queries,
                    new_key,
                    new_value,
                    key_cache,
                    value_cache,
                    out_weight,
                )
            ],
        )

    with jax.named_scope("exchange"):
        gathered = [messages[0]]
        for s in range(1, parts):
            gathered.append(
                lax.ppermute(
                    messages[s], "tensor", [(i, (i + s) % parts) for i in range(parts)]
                )
            )

    with jax.named_scope("load"):
        weight, _ = lax.optimization_barrier((out_weight, messages[0]))
        middle = pl.pallas_call(
            load_kernel,
            out_shape=pltpu.VMEM((depth, MIDDLE), bf16),
            in_specs=[ANY],
            out_specs=VM,
            scratch_shapes=[pltpu.SemaphoreType.DMA((MIDDLE // PIECE,))],
            compiler_params=pltpu.CompilerParams(vmem_limit_bytes=1 * MIB),
            cost_estimate=pl.CostEstimate(
                flops=0, bytes_accessed=2 * depth * MIDDLE, transcendentals=0
            ),
        )(in_hbm(weight))

    with jax.named_scope("project"):
        coded = pl.pallas_call(
            functools.partial(project_kernel, parts),
            out_shape=jax.ShapeDtypeStruct((row_count, width), bf16),
            in_specs=[VM] * (parts + 2) + [ANY, VM, VM],
            out_specs=VM,
            scratch_shapes=[
                pltpu.VMEM((depth, late), bf16),
                pltpu.VMEM((row_count, width), jnp.float32),
                pltpu.SemaphoreType.DMA((late // PIECE,)),
            ],
            compiler_params=pltpu.CompilerParams(vmem_limit_bytes=16 * MIB),
        )(*gathered, early, middle, in_hbm(out_weight), scale_row, hadamard)

    with jax.named_scope("reduce"):
        held = coded
        stride = 1
        while stride < parts:
            arrived = lax.ppermute(
                held, "tensor", [(i, i ^ stride) for i in range(parts)]
            )
            stride *= 2
            if stride < parts:
                held = (held.astype(jnp.float32) + arrived.astype(jnp.float32)).astype(
                    bf16
                )

    with jax.named_scope("finish"):
        return pl.pallas_call(
            finish_kernel,
            out_shape=[jax.ShapeDtypeStruct((row_count, width), bf16)] * 2,
            in_specs=[VM] * 6,
            out_specs=[VM] * 2,
            compiler_params=pltpu.CompilerParams(vmem_limit_bytes=16 * MIB),
        )(held, arrived, scale_row, hadamard, residual, gain_row)


def solution(mesh):
    placed = (
        P(("groups", "dp"), None),
        P(("groups", "dp"), "tensor", None),
        P(("groups", "dp"), "tensor", None),
        P(("groups", "dp"), None),
        P(("groups", "dp"), None),
        P(("groups", "dp")),
        P("tensor", None),
        P(),
        P(("groups", "dp"), None),
        P(),
    )
    return jax.shard_map(
        body,
        mesh=mesh,
        in_specs=placed,
        out_specs=(P(("groups", "dp"), None), P(("groups", "dp"), None)),
        check_vma=False,
    )
```

```python
import functools
import math

import jax
import jax.numpy as jnp
import numpy as np
from jax import lax
from jax.experimental import pallas as pl
from jax.experimental.pallas import tpu as pltpu
from jax.sharding import PartitionSpec as P

QH = 64
KVH = 8
HD = 128
HB = 64
GROUP = QH // KVH
TURN = 256
TERMS = 3
STATS = 32
EXTRA = 16

neg_fill = -1e30
coded_most = 448.0
norm_eps = 1e-05

PIECE = 512


def hadamard_tile():
    index = np.arange(TURN)
    both = (index[:, None] % HB) & (index[None, :] % HB)
    parity = np.zeros((TURN, TURN), np.int64)
    for bit in range(HB.bit_length() - 1):
        parity += (both >> bit) & 1
    signs = 1.0 - 2.0 * (parity % 2)
    same = (index[:, None] // HB) == (index[None, :] // HB)
    return np.where(same, signs, 0.0) / math.sqrt(HB)


def rotate(values, hadamard):
    rows, width = values.shape
    stacked = jnp.concatenate(
        [values[:, at : at + TURN] for at in range(0, width, TURN)], axis=0
    )
    high = stacked.astype(jnp.bfloat16)
    low = (stacked - high.astype(jnp.float32)).astype(jnp.bfloat16)
    turned = jnp.dot(high, hadamard, preferred_element_type=jnp.float32) + jnp.dot(
        low, hadamard, preferred_element_type=jnp.float32
    )
    return jnp.concatenate(
        [turned[at : at + rows] for at in range(0, turned.shape[0], rows)], axis=1
    )


def attend_kernel(
    parts,
    lengths_hbm,
    queries_hbm,
    new_key_hbm,
    new_value_hbm,
    key_hbm,
    value_hbm,
    weight_hbm,
    *refs,
):
    outs = refs[:parts]
    (
        lengths,
        queries,
        new_key,
        new_value,
        keys,
        values,
        q_rows,
        o_rows,
        small_sems,
        sems,
    ) = refs[parts:]
    row_count, places, _ = key_hbm.shape
    half = row_count // 2
    chunk = QH // parts * row_count
    me = lax.axis_index("tensor")
    scale = 1.0 / math.sqrt(HD)

    small = [
        pltpu.make_async_copy(queries_hbm, queries, small_sems.at[0]),
        pltpu.make_async_copy(lengths_hbm, lengths, small_sems.at[3]),
        pltpu.make_async_copy(new_key_hbm, new_key, small_sems.at[1]),
        pltpu.make_async_copy(new_value_hbm, new_value, small_sems.at[2]),
    ]
    for copy in small:
        copy.start()
    pairs = [(p, p + half) for p in range(half)]
    cached = pl.ds(0, places)
    key_copies = {}
    value_copies = {}
    G = row_count
    for r in range(0, row_count, G):
        key_copies[r] = pltpu.make_async_copy(
            key_hbm.at[r:r+G], keys.at[r:r+G, cached], sems.at[0, r]
        )
        key_copies[r].start()
    for r in range(0, row_count, G):
        value_copies[r] = pltpu.make_async_copy(
            value_hbm.at[r:r+G], values.at[r:r+G, cached], sems.at[1, r]
        )
        value_copies[r].start()

    for copy in small:
        copy.wait()
    for h in range(QH):
        q_rows[h * row_count : (h + 1) * row_count, :] = queries[
            :, h * HD : (h + 1) * HD
        ].astype(jnp.float32)
    extra = pl.ds(places, EXTRA)
    for r in range(row_count):
        wide = (EXTRA, KVH * HD)
        keys[r, extra, :] = jnp.broadcast_to(new_key[r : r + 1, :], wide)
        values[r, extra, :] = jnp.broadcast_to(new_value[r : r + 1, :], wide)

    lane = lax.broadcasted_iota(jnp.int32, (HD, 2 * QH), 1)
    place = lax.broadcasted_iota(jnp.int32, (places + EXTRA, 2 * QH), 0)
    lane_side = lax.broadcasted_iota(jnp.int32, (places + EXTRA, 2 * QH), 1) < QH
    place_end = jnp.where(me == 0, places + 1, places)
    for r in key_copies:
        key_copies[r].wait()
    scores = []
    for pair in pairs:
        both = jnp.concatenate(
            [q_rows[pl.ds(r, QH, stride=row_count), :] for r in pair], axis=0
        )
        turned = both.T
        score = 0.0
        for e, r in enumerate(pair):
            spread = jnp.concatenate(
                [
                    jnp.where(lane // GROUP == e * KVH + k, turned, 0.0)
                    for k in range(KVH)
                ],
                axis=0,
            ).astype(jnp.bfloat16)
            score = score + jnp.dot(
                keys[r], spread, preferred_element_type=jnp.float32
            )
        scores.append(score * scale)
    tops, sums, weights = [], [], []
    for pair, score in zip(pairs, scores):
        limit = [jnp.minimum(lengths[r] - me * places, places) for r in pair]
        valid = (place < jnp.where(lane_side, limit[0], limit[1])) | (
            (place >= places) & (place < place_end)
        )
        score = jnp.where(valid, score, neg_fill)
        top = jnp.max(score, axis=0, keepdims=True)
        weight = jnp.where(valid, jnp.exp(score - top), 0.0)
        tops.append(top)
        sums.append(jnp.sum(weight, axis=0, keepdims=True))
        weights.append(weight.T.astype(jnp.bfloat16))
    for r in value_copies:
        value_copies[r].wait()
    for pair, weight in zip(pairs, weights):
        for e, r in enumerate(pair):
            pieces = []
            for t in range(KVH // 2):
                at = e * QH + 2 * GROUP * t
                two = jnp.dot(
                    weight[at : at + 2 * GROUP],
                    values[r, :, 2 * HD * t : 2 * HD * (t + 1)],
                    preferred_element_type=jnp.float32,
                )
                pieces.append(two[:GROUP, :HD])
                pieces.append(two[GROUP:, HD:])
            o_rows[pl.ds(r, QH, stride=row_count), :] = jnp.concatenate(pieces, axis=0)

    def by_row(lines):
        lines = jnp.concatenate(lines, axis=0)
        return jnp.concatenate([lines[:, :QH], lines[:, QH:]], axis=0)

    rest = jnp.concatenate([by_row(tops), by_row(sums)], axis=1)
    terms = []
    for _ in range(TERMS):
        high = rest.astype(jnp.bfloat16).astype(jnp.float32)
        terms.append(high)
        rest = rest - high
    terms.append(jnp.zeros((STATS - TERMS * row_count, HD), jnp.float32))
    stats = jnp.concatenate(terms, axis=0).astype(jnp.bfloat16)
    for s in range(parts):
        to = me ^ s
        block = pl.ds(pl.multiple_of(to * chunk, chunk), chunk)
        outs[s][:chunk, :] = o_rows[block, :].astype(jnp.bfloat16)
        outs[s][chunk:, :] = stats


def project_kernel(parts, *refs):
    messages = refs[:parts]
    (
        weight,
        quant_scale,
        hadamard,
        coded,
        product,
    ) = refs[parts:]
    row_count = coded.shape[0]
    chunk = messages[0].shape[0] - STATS
    heads = chunk // row_count
    me = lax.axis_index("tensor")

    tops, sums = [], []
    for message in messages:
        lines = message[chunk:, :].astype(jnp.float32)
        lines = sum(lines[t * row_count : (t + 1) * row_count] for t in range(TERMS))
        tops.append(lines)
        sums.append(pltpu.roll(lines, QH, 1))
    top = functools.reduce(jnp.maximum, tops)
    factors = [jnp.exp(one - top) for one in tops]
    total = functools.reduce(jnp.add, [f * one for f, one in zip(factors, sums)])
    shares = [
        pltpu.roll(f / total, lax.rem(2 * QH - me * heads, 2 * QH), 1) for f in factors
    ]
    mixed = []
    for h in range(heads):
        at = slice(h * row_count, (h + 1) * row_count)
        mixed.append(
            functools.reduce(
                jnp.add,
                [
                    message[at, :].astype(jnp.float32) * share[:, h : h + 1]
                    for share, message in zip(shares, messages)
                ],
            )
        )
    attention = jnp.concatenate(mixed, axis=1).astype(jnp.bfloat16)

    for at in range(0, coded.shape[1], PIECE):
        product[:, at : at + PIECE] = jnp.dot(
            attention, weight[:, at : at + PIECE], preferred_element_type=jnp.float32
        )
    turned = rotate(product[...], hadamard[...])
    coded[...] = jnp.clip(turned / quant_scale[...], -coded_most, coded_most).astype(
        jnp.bfloat16
    )


def finish_kernel(
    mine, theirs, quant_scale, hadamard, residual, gain, new_residual, normed
):
    summed = mine[...].astype(jnp.float32) + theirs[...].astype(jnp.float32)
    restored = rotate(summed * quant_scale[...], hadamard[...])
    combined = residual[...].astype(jnp.float32) + restored
    mean_square = jnp.mean(combined * combined, axis=1, keepdims=True)
    new_residual[...] = combined.astype(jnp.bfloat16)
    normed[...] = (
        combined * lax.rsqrt(mean_square + norm_eps) * gain[...].astype(jnp.float32)
    ).astype(jnp.bfloat16)


VM = pl.BlockSpec(memory_space=pltpu.VMEM)
SM = pl.BlockSpec(memory_space=pltpu.SMEM)
ANY = pl.BlockSpec(memory_space=pl.ANY)
MIB = 1 << 20


def in_hbm(array):
    return pltpu.with_memory_space_constraint(array, pltpu.HBM)


def body(
    queries,
    key_cache,
    value_cache,
    new_key,
    new_value,
    lengths,
    out_weight,
    quant_scale,
    residual,
    norm_gain,
):
    row_count, places, kv_width = key_cache.shape
    parts = lax.axis_size("tensor")
    width = out_weight.shape[1]
    chunk = QH // parts * row_count
    hadamard = jnp.asarray(hadamard_tile(), jnp.bfloat16)
    scale_row = quant_scale.reshape(1, width)
    gain_row = norm_gain.reshape(1, width)
    bf16 = jnp.bfloat16

    with jax.named_scope("attend"):
        messages = pl.pallas_call(
            functools.partial(attend_kernel, parts),
            out_shape=[
                jax.ShapeDtypeStruct((chunk + STATS, HD), bf16) for _ in range(parts)
            ],
            in_specs=[ANY] * 7,
            out_specs=[VM] * parts,
            scratch_shapes=[
                pltpu.SMEM(lengths.shape, jnp.int32),
                pltpu.VMEM(queries.shape, bf16),
                pltpu.VMEM(new_key.shape, bf16),
                pltpu.VMEM(new_value.shape, bf16),
                pltpu.VMEM((row_count, places + EXTRA, kv_width), bf16),
                pltpu.VMEM((row_count, places + EXTRA, kv_width), bf16),
                pltpu.VMEM((QH * row_count, HD), jnp.float32),
                pltpu.VMEM((QH * row_count, HD), jnp.float32),
                pltpu.SemaphoreType.DMA((4,)),
                pltpu.SemaphoreType.DMA((2, row_count)),
            ],
            compiler_params=pltpu.CompilerParams(vmem_limit_bytes=12 * MIB),
        )(
            *[
                in_hbm(array)
                for array in (
                    lengths,
                    queries,
                    new_key,
                    new_value,
                    key_cache,
                    value_cache,
                    out_weight,
                )
            ],
        )

    with jax.named_scope("exchange"):
        gathered = [messages[0]]
        for s in [parts - 1, *range(1, parts - 1)]:
            gathered.append(
                lax.ppermute(
                    messages[s], "tensor", [(i, i ^ s) for i in range(parts)]
                )
            )

    with jax.named_scope("project"):
        coded = pl.pallas_call(
            functools.partial(project_kernel, parts),
            out_shape=jax.ShapeDtypeStruct((row_count, width), bf16),
            in_specs=[VM] * (parts + 3),
            out_specs=VM,
            scratch_shapes=[
                pltpu.VMEM((row_count, width), jnp.float32),
            ],
            compiler_params=pltpu.CompilerParams(vmem_limit_bytes=16 * MIB),
        )(
            *gathered,
            pltpu.with_memory_space_constraint(out_weight, pltpu.VMEM),
            scale_row,
            hadamard,
        )

    with jax.named_scope("reduce"):
        held = coded
        stride = 1
        while stride < parts:
            arrived = lax.ppermute(
                held, "tensor", [(i, i ^ stride) for i in range(parts)]
            )
            stride *= 2
            if stride < parts:
                held = (held.astype(jnp.float32) + arrived.astype(jnp.float32)).astype(
                    bf16
                )

    with jax.named_scope("finish"):
        return pl.pallas_call(
            finish_kernel,
            out_shape=[jax.ShapeDtypeStruct((row_count, width), bf16)] * 2,
            in_specs=[VM] * 6,
            out_specs=[VM] * 2,
            compiler_params=pltpu.CompilerParams(vmem_limit_bytes=16 * MIB),
        )(held, arrived, scale_row, hadamard, residual, gain_row)


def solution(mesh):
    placed = (
        P(("groups", "dp"), None),
        P(("groups", "dp"), "tensor", None),
        P(("groups", "dp"), "tensor", None),
        P(("groups", "dp"), None),
        P(("groups", "dp"), None),
        P(("groups", "dp")),
        P("tensor", None),
        P(),
        P(("groups", "dp"), None),
        P(),
    )
    return jax.shard_map(
        body,
        mesh=mesh,
        in_specs=placed,
        out_specs=(P(("groups", "dp"), None), P(("groups", "dp"), None)),
        check_vma=False,
    )
```

```python
import functools
import math

import jax
import jax.numpy as jnp
import numpy as np
from jax import lax
from jax.experimental import pallas as pl
from jax.experimental.pallas import tpu as pltpu
from jax.sharding import PartitionSpec as P

QH = 64
KVH = 8
HD = 128
HB = 64
GROUP = QH // KVH
TURN = 256
TERMS = 3
STATS = 32
EXTRA = 16

neg_fill = -1e30
coded_most = 448.0
norm_eps = 1e-05

PIECE = 512


def hadamard_tile():
    index = np.arange(TURN)
    both = (index[:, None] % HB) & (index[None, :] % HB)
    parity = np.zeros((TURN, TURN), np.int64)
    for bit in range(HB.bit_length() - 1):
        parity += (both >> bit) & 1
    signs = 1.0 - 2.0 * (parity % 2)
    same = (index[:, None] // HB) == (index[None, :] // HB)
    return np.where(same, signs, 0.0) / math.sqrt(HB)


def rotate(values, hadamard):
    rows, width = values.shape
    stacked = jnp.concatenate(
        [values[:, at : at + TURN] for at in range(0, width, TURN)], axis=0
    )
    high = stacked.astype(jnp.bfloat16)
    low = (stacked - high.astype(jnp.float32)).astype(jnp.bfloat16)
    turned = jnp.dot(high, hadamard, preferred_element_type=jnp.float32) + jnp.dot(
        low, hadamard, preferred_element_type=jnp.float32
    )
    return jnp.concatenate(
        [turned[at : at + rows] for at in range(0, turned.shape[0], rows)], axis=1
    )


def attend_kernel(
    parts,
    lengths_hbm,
    queries_hbm,
    new_key_hbm,
    new_value_hbm,
    key_hbm,
    value_hbm,
    weight_hbm,
    *refs,
):
    outs = refs[:parts]
    (
        lengths,
        queries,
        new_key,
        new_value,
        keys,
        values,
        q_rows,
        o_rows,
        small_sems,
        sems,
    ) = refs[parts:]
    row_count, places, _ = key_hbm.shape
    half = row_count // 2
    chunk = QH // parts * row_count
    me = lax.axis_index("tensor")
    scale = 1.0 / math.sqrt(HD)

    small = [
        pltpu.make_async_copy(queries_hbm, queries, small_sems.at[0]),
        pltpu.make_async_copy(lengths_hbm, lengths, small_sems.at[3]),
        pltpu.make_async_copy(new_key_hbm, new_key, small_sems.at[1]),
        pltpu.make_async_copy(new_value_hbm, new_value, small_sems.at[2]),
    ]
    for copy in small:
        copy.start()
    pairs = [(p, p + half) for p in range(half)]
    cached = pl.ds(0, places)
    key_copies = {}
    value_copies = {}
    G = row_count
    for r in range(0, row_count, G):
        key_copies[r] = pltpu.make_async_copy(
            key_hbm.at[r:r+G], keys.at[r:r+G, cached], sems.at[0, r]
        )
        key_copies[r].start()
    for r in range(0, row_count, G):
        value_copies[r] = pltpu.make_async_copy(
            value_hbm.at[r:r+G], values.at[r:r+G, cached], sems.at[1, r]
        )
        value_copies[r].start()

    for copy in small:
        copy.wait()
    for h in range(QH):
        q_rows[h * row_count : (h + 1) * row_count, :] = queries[
            :, h * HD : (h + 1) * HD
        ].astype(jnp.float32)
    extra = pl.ds(places, EXTRA)
    for r in range(row_count):
        wide = (EXTRA, KVH * HD)
        keys[r, extra, :] = jnp.broadcast_to(new_key[r : r + 1, :], wide)
        values[r, extra, :] = jnp.broadcast_to(new_value[r : r + 1, :], wide)

    lane = lax.broadcasted_iota(jnp.int32, (HD, 2 * QH), 1)
    place = lax.broadcasted_iota(jnp.int32, (places + EXTRA, 2 * QH), 0)
    lane_side = lax.broadcasted_iota(jnp.int32, (places + EXTRA, 2 * QH), 1) < QH
    place_end = jnp.where(me == 0, places + 1, places)
    for r in key_copies:
        key_copies[r].wait()
    scores = []
    for pair in pairs:
        both = jnp.concatenate(
            [q_rows[pl.ds(r, QH, stride=row_count), :] for r in pair], axis=0
        )
        turned = both.T
        score = 0.0
        for e, r in enumerate(pair):
            spread = jnp.concatenate(
                [
                    jnp.where(lane // GROUP == e * KVH + k, turned, 0.0)
                    for k in range(KVH)
                ],
                axis=0,
            ).astype(jnp.bfloat16)
            score = score + jnp.dot(
                keys[r], spread, preferred_element_type=jnp.float32
            )
        scores.append(score * scale)
    tops, sums, weights = [], [], []
    for pair, score in zip(pairs, scores):
        limit = [jnp.minimum(lengths[r] - me * places, places) for r in pair]
        valid = (place < jnp.where(lane_side, limit[0], limit[1])) | (
            (place >= places) & (place < place_end)
        )
        score = jnp.where(valid, score, neg_fill)
        top = jnp.max(score, axis=0, keepdims=True)
        weight = jnp.where(valid, jnp.exp(score - top), 0.0)
        tops.append(top)
        sums.append(jnp.sum(weight, axis=0, keepdims=True))
        weights.append(weight.T.astype(jnp.bfloat16))
    for r in value_copies:
        value_copies[r].wait()
    for pair, weight in zip(pairs, weights):
        for e, r in enumerate(pair):
            pieces = []
            for t in range(KVH // 2):
                at = e * QH + 2 * GROUP * t
                two = jnp.dot(
                    weight[at : at + 2 * GROUP],
                    values[r, :, 2 * HD * t : 2 * HD * (t + 1)],
                    preferred_element_type=jnp.float32,
                )
                pieces.append(two[:GROUP, :HD])
                pieces.append(two[GROUP:, HD:])
            o_rows[pl.ds(r, QH, stride=row_count), :] = jnp.concatenate(pieces, axis=0)

    def by_row(lines):
        lines = jnp.concatenate(lines, axis=0)
        return jnp.concatenate([lines[:, :QH], lines[:, QH:]], axis=0)

    rest = jnp.concatenate([by_row(tops), by_row(sums)], axis=1)
    terms = []
    for _ in range(TERMS):
        high = rest.astype(jnp.bfloat16).astype(jnp.float32)
        terms.append(high)
        rest = rest - high
    terms.append(jnp.zeros((STATS - TERMS * row_count, HD), jnp.float32))
    stats = jnp.concatenate(terms, axis=0).astype(jnp.bfloat16)
    for s in range(parts):
        to = me ^ s
        block = pl.ds(pl.multiple_of(to * chunk, chunk), chunk)
        outs[s][:chunk, :] = o_rows[block, :].astype(jnp.bfloat16)
        outs[s][chunk:, :] = stats


def project_kernel(parts, *refs):
    messages = refs[:parts]
    (
        weight,
        quant_scale,
        hadamard,
        coded,
        product,
    ) = refs[parts:]
    row_count = coded.shape[0]
    chunk = messages[0].shape[0] - STATS
    heads = chunk // row_count
    me = lax.axis_index("tensor")

    tops, sums = [], []
    for message in messages:
        lines = message[chunk:, :].astype(jnp.float32)
        lines = sum(lines[t * row_count : (t + 1) * row_count] for t in range(TERMS))
        tops.append(lines)
        sums.append(pltpu.roll(lines, QH, 1))
    top = functools.reduce(jnp.maximum, tops)
    factors = [jnp.exp(one - top) for one in tops]
    total = functools.reduce(jnp.add, [f * one for f, one in zip(factors, sums)])
    shares = [
        pltpu.roll(f / total, lax.rem(2 * QH - me * heads, 2 * QH), 1) for f in factors
    ]
    mixed = []
    for h in range(heads):
        at = slice(h * row_count, (h + 1) * row_count)
        mixed.append(
            functools.reduce(
                jnp.add,
                [
                    message[at, :].astype(jnp.float32) * share[:, h : h + 1]
                    for share, message in zip(shares, messages)
                ],
            )
        )
    attention = jnp.concatenate(mixed, axis=1).astype(jnp.bfloat16)

    for at in range(0, coded.shape[1], PIECE):
        product[:, at : at + PIECE] = jnp.dot(
            attention, weight[:, at : at + PIECE], preferred_element_type=jnp.float32
        )
    turned = rotate(product[...], hadamard[...])
    coded[...] = jnp.clip(turned / quant_scale[...], -coded_most, coded_most).astype(
        jnp.bfloat16
    )


def finish_kernel(*refs):
    *terms, quant_scale, hadamard, residual, gain, new_residual, normed = refs
    summed = functools.reduce(jnp.add, [t[...].astype(jnp.float32) for t in terms])
    restored = rotate(summed * quant_scale[...], hadamard[...])
    combined = residual[...].astype(jnp.float32) + restored
    mean_square = jnp.mean(combined * combined, axis=1, keepdims=True)
    new_residual[...] = combined.astype(jnp.bfloat16)
    normed[...] = (
        combined * lax.rsqrt(mean_square + norm_eps) * gain[...].astype(jnp.float32)
    ).astype(jnp.bfloat16)


VM = pl.BlockSpec(memory_space=pltpu.VMEM)
SM = pl.BlockSpec(memory_space=pltpu.SMEM)
ANY = pl.BlockSpec(memory_space=pl.ANY)
MIB = 1 << 20


def in_hbm(array):
    return pltpu.with_memory_space_constraint(array, pltpu.HBM)


def body(
    queries,
    key_cache,
    value_cache,
    new_key,
    new_value,
    lengths,
    out_weight,
    quant_scale,
    residual,
    norm_gain,
):
    row_count, places, kv_width = key_cache.shape
    parts = lax.axis_size("tensor")
    width = out_weight.shape[1]
    chunk = QH // parts * row_count
    hadamard = jnp.asarray(hadamard_tile(), jnp.bfloat16)
    scale_row = quant_scale.reshape(1, width)
    gain_row = norm_gain.reshape(1, width)
    bf16 = jnp.bfloat16

    with jax.named_scope("attend"):
        messages = pl.pallas_call(
            functools.partial(attend_kernel, parts),
            out_shape=[
                jax.ShapeDtypeStruct((chunk + STATS, HD), bf16) for _ in range(parts)
            ],
            in_specs=[ANY] * 7,
            out_specs=[VM] * parts,
            scratch_shapes=[
                pltpu.SMEM(lengths.shape, jnp.int32),
                pltpu.VMEM(queries.shape, bf16),
                pltpu.VMEM(new_key.shape, bf16),
                pltpu.VMEM(new_value.shape, bf16),
                pltpu.VMEM((row_count, places + EXTRA, kv_width), bf16),
                pltpu.VMEM((row_count, places + EXTRA, kv_width), bf16),
                pltpu.VMEM((QH * row_count, HD), jnp.float32),
                pltpu.VMEM((QH * row_count, HD), jnp.float32),
                pltpu.SemaphoreType.DMA((4,)),
                pltpu.SemaphoreType.DMA((2, row_count)),
            ],
            compiler_params=pltpu.CompilerParams(vmem_limit_bytes=12 * MIB),
        )(
            *[
                in_hbm(array)
                for array in (
                    lengths,
                    queries,
                    new_key,
                    new_value,
                    key_cache,
                    value_cache,
                    out_weight,
                )
            ],
        )

    partners = [parts - 1, *range(1, parts - 1)]

    def from_partner(array, s):
        return lax.ppermute(array, "tensor", [(i, i ^ s) for i in range(parts)])

    with jax.named_scope("exchange"):
        gathered = [messages[0]] + [from_partner(messages[s], s) for s in partners]

    with jax.named_scope("project"):
        coded = pl.pallas_call(
            functools.partial(project_kernel, parts),
            out_shape=jax.ShapeDtypeStruct((row_count, width), bf16),
            in_specs=[VM] * (parts + 3),
            out_specs=VM,
            scratch_shapes=[
                pltpu.VMEM((row_count, width), jnp.float32),
            ],
            compiler_params=pltpu.CompilerParams(vmem_limit_bytes=16 * MIB),
        )(
            *gathered,
            pltpu.with_memory_space_constraint(out_weight, pltpu.VMEM),
            scale_row,
            hadamard,
        )

    with jax.named_scope("reduce"):
        terms = [coded] + [from_partner(coded, s) for s in partners]

    with jax.named_scope("finish"):
        return pl.pallas_call(
            finish_kernel,
            out_shape=[jax.ShapeDtypeStruct((row_count, width), bf16)] * 2,
            in_specs=[VM] * (parts + 4),
            out_specs=[VM] * 2,
            compiler_params=pltpu.CompilerParams(vmem_limit_bytes=16 * MIB),
        )(*terms, scale_row, hadamard, residual, gain_row)


def solution(mesh):
    placed = (
        P(("groups", "dp"), None),
        P(("groups", "dp"), "tensor", None),
        P(("groups", "dp"), "tensor", None),
        P(("groups", "dp"), None),
        P(("groups", "dp"), None),
        P(("groups", "dp")),
        P("tensor", None),
        P(),
        P(("groups", "dp"), None),
        P(),
    )
    return jax.shard_map(
        body,
        mesh=mesh,
        in_specs=placed,
        out_specs=(P(("groups", "dp"), None), P(("groups", "dp"), None)),
        check_vma=False,
    )
```

```python
import functools
import math

import jax
import jax.numpy as jnp
import numpy as np
from jax import lax
from jax.experimental import pallas as pl
from jax.experimental.pallas import tpu as pltpu
from jax.sharding import PartitionSpec as P

QH = 64
KVH = 8
HD = 128
HB = 64
GROUP = QH // KVH
TURN = 256
TERMS = 3
STATS = 32
EXTRA = 16

neg_fill = -1e30
coded_most = 448.0
norm_eps = 1e-05

PIECE = 512


def hadamard_tile():
    index = np.arange(TURN)
    both = (index[:, None] % HB) & (index[None, :] % HB)
    parity = np.zeros((TURN, TURN), np.int64)
    for bit in range(HB.bit_length() - 1):
        parity += (both >> bit) & 1
    signs = 1.0 - 2.0 * (parity % 2)
    same = (index[:, None] // HB) == (index[None, :] // HB)
    return np.where(same, signs, 0.0) / math.sqrt(HB)


def rotate(values, hadamard):
    rows, width = values.shape
    stacked = jnp.concatenate(
        [values[:, at : at + TURN] for at in range(0, width, TURN)], axis=0
    )
    high = stacked.astype(jnp.bfloat16)
    low = (stacked - high.astype(jnp.float32)).astype(jnp.bfloat16)
    turned = jnp.dot(high, hadamard, preferred_element_type=jnp.float32) + jnp.dot(
        low, hadamard, preferred_element_type=jnp.float32
    )
    return jnp.concatenate(
        [turned[at : at + rows] for at in range(0, turned.shape[0], rows)], axis=1
    )


def attend_kernel(
    parts,
    lengths_hbm,
    queries_hbm,
    new_key_hbm,
    new_value_hbm,
    key_hbm,
    value_hbm,
    weight_hbm,
    *refs,
):
    outs = refs[:parts]
    (
        lengths,
        queries,
        new_key,
        new_value,
        keys,
        values,
        q_rows,
        o_rows,
        small_sems,
        sems,
    ) = refs[parts:]
    row_count, places, _ = key_hbm.shape
    half = row_count // 2
    chunk = QH // parts * row_count
    me = lax.axis_index("tensor")
    scale = 1.0 / math.sqrt(HD)

    small = [
        pltpu.make_async_copy(queries_hbm, queries, small_sems.at[0]),
        pltpu.make_async_copy(lengths_hbm, lengths, small_sems.at[3]),
        pltpu.make_async_copy(new_key_hbm, new_key, small_sems.at[1]),
        pltpu.make_async_copy(new_value_hbm, new_value, small_sems.at[2]),
    ]
    for copy in small:
        copy.start()
    pairs = [(p, p + half) for p in range(half)]
    cached = pl.ds(0, places)
    key_copies = {}
    value_copies = {}
    G = row_count
    for r in range(0, row_count, G):
        key_copies[r] = pltpu.make_async_copy(
            key_hbm.at[r:r+G], keys.at[r:r+G, cached], sems.at[0, r]
        )
        key_copies[r].start()
    for r in range(0, row_count, G):
        value_copies[r] = pltpu.make_async_copy(
            value_hbm.at[r:r+G], values.at[r:r+G, cached], sems.at[1, r]
        )
        value_copies[r].start()

    for copy in small:
        copy.wait()
    for h in range(QH):
        q_rows[h * row_count : (h + 1) * row_count, :] = queries[
            :, h * HD : (h + 1) * HD
        ].astype(jnp.float32)
    extra = pl.ds(places, EXTRA)
    for r in range(row_count):
        wide = (EXTRA, KVH * HD)
        keys[r, extra, :] = jnp.broadcast_to(new_key[r : r + 1, :], wide)
        values[r, extra, :] = jnp.broadcast_to(new_value[r : r + 1, :], wide)

    lane = lax.broadcasted_iota(jnp.int32, (HD, 2 * QH), 1)
    place = lax.broadcasted_iota(jnp.int32, (places + EXTRA, 2 * QH), 0)
    lane_side = lax.broadcasted_iota(jnp.int32, (places + EXTRA, 2 * QH), 1) < QH
    place_end = jnp.where(me == 0, places + 1, places)
    for r in key_copies:
        key_copies[r].wait()
    scores = []
    for pair in pairs:
        both = jnp.concatenate(
            [q_rows[pl.ds(r, QH, stride=row_count), :] for r in pair], axis=0
        )
        turned = both.T
        score = 0.0
        for e, r in enumerate(pair):
            spread = jnp.concatenate(
                [
                    jnp.where(lane // GROUP == e * KVH + k, turned, 0.0)
                    for k in range(KVH)
                ],
                axis=0,
            ).astype(jnp.bfloat16)
            score = score + jnp.dot(
                keys[r], spread, preferred_element_type=jnp.float32
            )
        scores.append(score * scale)
    tops, sums, weights = [], [], []
    for pair, score in zip(pairs, scores):
        limit = [jnp.minimum(lengths[r] - me * places, places) for r in pair]
        valid = (place < jnp.where(lane_side, limit[0], limit[1])) | (
            (place >= places) & (place < place_end)
        )
        score = jnp.where(valid, score, neg_fill)
        top = jnp.max(score, axis=0, keepdims=True)
        weight = jnp.where(valid, jnp.exp(score - top), 0.0)
        tops.append(top)
        sums.append(jnp.sum(weight, axis=0, keepdims=True))
        weights.append(weight.T.astype(jnp.bfloat16))
    for r in value_copies:
        value_copies[r].wait()
    for pair, weight in zip(pairs, weights):
        for e, r in enumerate(pair):
            pieces = []
            for t in range(KVH // 2):
                at = e * QH + 2 * GROUP * t
                two = jnp.dot(
                    weight[at : at + 2 * GROUP],
                    values[r, :, 2 * HD * t : 2 * HD * (t + 1)],
                    preferred_element_type=jnp.float32,
                )
                pieces.append(two[:GROUP, :HD])
                pieces.append(two[GROUP:, HD:])
            o_rows[pl.ds(r, QH, stride=row_count), :] = jnp.concatenate(pieces, axis=0)

    def by_row(lines):
        lines = jnp.concatenate(lines, axis=0)
        return jnp.concatenate([lines[:, :QH], lines[:, QH:]], axis=0)

    rest = jnp.concatenate([by_row(tops), by_row(sums)], axis=1)
    terms = []
    for _ in range(TERMS):
        high = rest.astype(jnp.bfloat16).astype(jnp.float32)
        terms.append(high)
        rest = rest - high
    terms.append(jnp.zeros((STATS - TERMS * row_count, HD), jnp.float32))
    stats = jnp.concatenate(terms, axis=0).astype(jnp.bfloat16)
    for s in range(parts):
        to = me ^ s
        block = pl.ds(pl.multiple_of(to * chunk, chunk), chunk)
        outs[s][:chunk, :] = o_rows[block, :].astype(jnp.bfloat16)
        outs[s][chunk:, :] = stats


def project_kernel(parts, *refs):
    messages = refs[:parts]
    (
        weight,
        quant_scale,
        hadamard,
        coded,
        product,
    ) = refs[parts:]
    row_count = coded.shape[0]
    chunk = messages[0].shape[0] - STATS
    heads = chunk // row_count
    me = lax.axis_index("tensor")

    tops, sums = [], []
    for message in messages:
        lines = message[chunk:, :].astype(jnp.float32)
        lines = sum(lines[t * row_count : (t + 1) * row_count] for t in range(TERMS))
        tops.append(lines)
        sums.append(pltpu.roll(lines, QH, 1))
    top = functools.reduce(jnp.maximum, tops)
    factors = [jnp.exp(one - top) for one in tops]
    total = functools.reduce(jnp.add, [f * one for f, one in zip(factors, sums)])
    shares = [
        pltpu.roll(f / total, lax.rem(2 * QH - me * heads, 2 * QH), 1) for f in factors
    ]
    mixed = []
    for h in range(heads):
        at = slice(h * row_count, (h + 1) * row_count)
        mixed.append(
            functools.reduce(
                jnp.add,
                [
                    message[at, :].astype(jnp.float32) * share[:, h : h + 1]
                    for share, message in zip(shares, messages)
                ],
            )
        )
    attention = jnp.concatenate(mixed, axis=1).astype(jnp.bfloat16)

    for at in range(0, coded.shape[1], PIECE):
        product[:, at : at + PIECE] = jnp.dot(
            attention, weight[:, at : at + PIECE], preferred_element_type=jnp.float32
        )
    turned = rotate(product[...], hadamard[...])
    coded[...] = jnp.clip(turned / quant_scale[...], -coded_most, coded_most).astype(
        jnp.bfloat16
    )


def finish_kernel(*refs):
    *terms, quant_scale, hadamard, residual, gain, new_residual, normed = refs
    summed = functools.reduce(jnp.add, [t[...].astype(jnp.float32) for t in terms])
    restored = rotate(summed * quant_scale[...], hadamard[...])
    combined = residual[...].astype(jnp.float32) + restored
    mean_square = jnp.mean(combined * combined, axis=1, keepdims=True)
    new_residual[...] = combined.astype(jnp.bfloat16)
    normed[...] = (
        combined * lax.rsqrt(mean_square + norm_eps) * gain[...].astype(jnp.float32)
    ).astype(jnp.bfloat16)


VM = pl.BlockSpec(memory_space=pltpu.VMEM)
SM = pl.BlockSpec(memory_space=pltpu.SMEM)
ANY = pl.BlockSpec(memory_space=pl.ANY)
MIB = 1 << 20


def in_hbm(array):
    return pltpu.with_memory_space_constraint(array, pltpu.HBM)


def body(
    queries,
    key_cache,
    value_cache,
    new_key,
    new_value,
    lengths,
    out_weight,
    quant_scale,
    residual,
    norm_gain,
):
    row_count, places, kv_width = key_cache.shape
    parts = lax.axis_size("tensor")
    width = out_weight.shape[1]
    chunk = QH // parts * row_count
    hadamard = jnp.asarray(hadamard_tile(), jnp.bfloat16)
    scale_row = quant_scale.reshape(1, width)
    gain_row = norm_gain.reshape(1, width)
    bf16 = jnp.bfloat16

    with jax.named_scope("attend"):
        messages = pl.pallas_call(
            functools.partial(attend_kernel, parts),
            out_shape=[
                jax.ShapeDtypeStruct((chunk + STATS, HD), bf16) for _ in range(parts)
            ],
            in_specs=[ANY] * 7,
            out_specs=[VM] * parts,
            scratch_shapes=[
                pltpu.SMEM(lengths.shape, jnp.int32),
                pltpu.VMEM(queries.shape, bf16),
                pltpu.VMEM(new_key.shape, bf16),
                pltpu.VMEM(new_value.shape, bf16),
                pltpu.VMEM((row_count, places + EXTRA, kv_width), bf16),
                pltpu.VMEM((row_count, places + EXTRA, kv_width), bf16),
                pltpu.VMEM((QH * row_count, HD), jnp.float32),
                pltpu.VMEM((QH * row_count, HD), jnp.float32),
                pltpu.SemaphoreType.DMA((4,)),
                pltpu.SemaphoreType.DMA((2, row_count)),
            ],
            compiler_params=pltpu.CompilerParams(vmem_limit_bytes=12 * MIB),
        )(
            *[
                in_hbm(array)
                for array in (
                    lengths,
                    queries,
                    new_key,
                    new_value,
                    key_cache,
                    value_cache,
                    out_weight,
                )
            ],
        )

    def paired(array, s):
        return lax.ppermute(array, "tensor", [(i, i ^ s) for i in range(parts)])

    def shifted(array, s):
        return lax.ppermute(
            array, "tensor", [(i, (i + s) % parts) for i in range(parts)]
        )

    with jax.named_scope("exchange"):
        half = parts // 2
        order = [*range(half, parts), *range(1, half)]
        gathered = [messages[0]] + [paired(messages[s], s) for s in order]

    with jax.named_scope("project"):
        coded = pl.pallas_call(
            functools.partial(project_kernel, parts),
            out_shape=jax.ShapeDtypeStruct((row_count, width), bf16),
            in_specs=[VM] * (parts + 3),
            out_specs=VM,
            scratch_shapes=[
                pltpu.VMEM((row_count, width), jnp.float32),
            ],
            compiler_params=pltpu.CompilerParams(vmem_limit_bytes=16 * MIB),
        )(
            *gathered,
            pltpu.with_memory_space_constraint(out_weight, pltpu.VMEM),
            scale_row,
            hadamard,
        )

    with jax.named_scope("reduce"):
        order = [parts - 1, *range(1, parts - 1)]
        terms = [coded] + [shifted(coded, s) for s in order]

    with jax.named_scope("finish"):
        return pl.pallas_call(
            finish_kernel,
            out_shape=[jax.ShapeDtypeStruct((row_count, width), bf16)] * 2,
            in_specs=[VM] * (parts + 4),
            out_specs=[VM] * 2,
            compiler_params=pltpu.CompilerParams(vmem_limit_bytes=16 * MIB),
        )(*terms, scale_row, hadamard, residual, gain_row)


def solution(mesh):
    placed = (
        P(("groups", "dp"), None),
        P(("groups", "dp"), "tensor", None),
        P(("groups", "dp"), "tensor", None),
        P(("groups", "dp"), None),
        P(("groups", "dp"), None),
        P(("groups", "dp")),
        P("tensor", None),
        P(),
        P(("groups", "dp"), None),
        P(),
    )
    return jax.shard_map(
        body,
        mesh=mesh,
        in_specs=placed,
        out_specs=(P(("groups", "dp"), None), P(("groups", "dp"), None)),
        check_vma=False,
    )
```

```python
import functools
import math

import jax
import jax.numpy as jnp
import numpy as np
from jax import lax
from jax.experimental import pallas as pl
from jax.experimental.pallas import tpu as pltpu
from jax.sharding import PartitionSpec as P

QH = 64
KVH = 8
HD = 128
HB = 64
GROUP = QH // KVH
TURN = 256
TERMS = 3
STATS = 32
EXTRA = 16

neg_fill = -1e30
coded_most = 448.0
norm_eps = 1e-05

PIECE = 512


def hadamard_tile():
    index = np.arange(TURN)
    both = (index[:, None] % HB) & (index[None, :] % HB)
    parity = np.zeros((TURN, TURN), np.int64)
    for bit in range(HB.bit_length() - 1):
        parity += (both >> bit) & 1
    signs = 1.0 - 2.0 * (parity % 2)
    same = (index[:, None] // HB) == (index[None, :] // HB)
    return np.where(same, signs, 0.0) / math.sqrt(HB)


def rotate(values, hadamard):
    rows, width = values.shape
    stacked = jnp.concatenate(
        [values[:, at : at + TURN] for at in range(0, width, TURN)], axis=0
    )
    high = stacked.astype(jnp.bfloat16)
    low = (stacked - high.astype(jnp.float32)).astype(jnp.bfloat16)
    turned = jnp.dot(high, hadamard, preferred_element_type=jnp.float32) + jnp.dot(
        low, hadamard, preferred_element_type=jnp.float32
    )
    return jnp.concatenate(
        [turned[at : at + rows] for at in range(0, turned.shape[0], rows)], axis=1
    )


def attend_kernel(
    parts,
    lengths_hbm,
    queries_hbm,
    new_key_hbm,
    new_value_hbm,
    key_hbm,
    value_hbm,
    weight_hbm,
    *refs,
):
    outs = refs[:parts]
    (
        lengths,
        queries,
        new_key,
        new_value,
        keys,
        values,
        q_rows,
        o_rows,
        small_sems,
        sems,
    ) = refs[parts:]
    row_count, places, _ = key_hbm.shape
    half = row_count // 2
    chunk = QH // parts * row_count
    me = lax.axis_index("tensor")
    scale = 1.0 / math.sqrt(HD)

    small = [
        pltpu.make_async_copy(queries_hbm, queries, small_sems.at[0]),
        pltpu.make_async_copy(lengths_hbm, lengths, small_sems.at[3]),
        pltpu.make_async_copy(new_key_hbm, new_key, small_sems.at[1]),
        pltpu.make_async_copy(new_value_hbm, new_value, small_sems.at[2]),
    ]
    for copy in small:
        copy.start()
    pairs = [(2 * p, 2 * p + 1) for p in range(half)]
    cached = pl.ds(0, places)
    key_copies = []
    for start in (0, half):
        rows = pl.ds(start, half)
        key_copies.append(
            pltpu.make_async_copy(
                key_hbm.at[rows], keys.at[rows, cached], sems.at[len(key_copies)]
            )
        )
        key_copies[-1].start()
    value_copy = pltpu.make_async_copy(value_hbm, values.at[:, cached], sems.at[2])
    value_copy.start()

    for copy in small:
        copy.wait()
    for h in range(QH):
        q_rows[h * row_count : (h + 1) * row_count, :] = queries[
            :, h * HD : (h + 1) * HD
        ].astype(jnp.float32)
    extra = pl.ds(places, EXTRA)
    for r in range(row_count):
        wide = (EXTRA, KVH * HD)
        keys[r, extra, :] = jnp.broadcast_to(new_key[r : r + 1, :], wide)
        values[r, extra, :] = jnp.broadcast_to(new_value[r : r + 1, :], wide)

    lane = lax.broadcasted_iota(jnp.int32, (HD, 2 * QH), 1)
    place = lax.broadcasted_iota(jnp.int32, (places + EXTRA, 2 * QH), 0)
    lane_side = lax.broadcasted_iota(jnp.int32, (places + EXTRA, 2 * QH), 1) < QH
    place_end = jnp.where(me == 0, places + 1, places)
    scores = []
    for p, pair in enumerate(pairs):
        if 2 * p % half == 0:
            key_copies[2 * p // half].wait()
        both = jnp.concatenate(
            [q_rows[pl.ds(r, QH, stride=row_count), :] for r in pair], axis=0
        )
        turned = both.T
        score = 0.0
        for e, r in enumerate(pair):
            spread = jnp.concatenate(
                [
                    jnp.where(lane // GROUP == e * KVH + k, turned, 0.0)
                    for k in range(KVH)
                ],
                axis=0,
            ).astype(jnp.bfloat16)
            score = score + jnp.dot(
                keys[r], spread, preferred_element_type=jnp.float32
            )
        scores.append(score * scale)
    tops, sums, weights = [], [], []
    for pair, score in zip(pairs, scores):
        limit = [jnp.minimum(lengths[r] - me * places, places) for r in pair]
        valid = (place < jnp.where(lane_side, limit[0], limit[1])) | (
            (place >= places) & (place < place_end)
        )
        score = jnp.where(valid, score, neg_fill)
        top = jnp.max(score, axis=0, keepdims=True)
        weight = jnp.where(valid, jnp.exp(score - top), 0.0)
        tops.append(top)
        sums.append(jnp.sum(weight, axis=0, keepdims=True))
        weights.append(weight.T.astype(jnp.bfloat16))
    value_copy.wait()
    for pair, weight in zip(pairs, weights):
        for e, r in enumerate(pair):
            pieces = []
            for t in range(KVH // 2):
                at = e * QH + 2 * GROUP * t
                two = jnp.dot(
                    weight[at : at + 2 * GROUP],
                    values[r, :, 2 * HD * t : 2 * HD * (t + 1)],
                    preferred_element_type=jnp.float32,
                )
                pieces.append(two[:GROUP, :HD])
                pieces.append(two[GROUP:, HD:])
            o_rows[pl.ds(r, QH, stride=row_count), :] = jnp.concatenate(pieces, axis=0)

    def by_row(lines):
        lines = jnp.concatenate(lines, axis=0)
        sides = (lines[:, :QH], lines[:, QH:])
        return jnp.concatenate(
            [side[p : p + 1] for p in range(half) for side in sides], axis=0
        )

    rest = jnp.concatenate([by_row(tops), by_row(sums)], axis=1)
    terms = []
    for _ in range(TERMS):
        high = rest.astype(jnp.bfloat16).astype(jnp.float32)
        terms.append(high)
        rest = rest - high
    terms.append(jnp.zeros((STATS - TERMS * row_count, HD), jnp.float32))
    stats = jnp.concatenate(terms, axis=0).astype(jnp.bfloat16)
    for s in range(parts):
        to = me ^ s
        block = pl.ds(pl.multiple_of(to * chunk, chunk), chunk)
        outs[s][:chunk, :] = o_rows[block, :].astype(jnp.bfloat16)
        outs[s][chunk:, :] = stats


def project_kernel(parts, *refs):
    messages = refs[:parts]
    (
        weight,
        quant_scale,
        hadamard,
        coded,
        product,
    ) = refs[parts:]
    row_count = coded.shape[0]
    chunk = messages[0].shape[0] - STATS
    heads = chunk // row_count
    me = lax.axis_index("tensor")

    tops, sums = [], []
    for message in messages:
        lines = message[chunk:, :].astype(jnp.float32)
        lines = sum(lines[t * row_count : (t + 1) * row_count] for t in range(TERMS))
        tops.append(lines)
        sums.append(pltpu.roll(lines, QH, 1))
    top = functools.reduce(jnp.maximum, tops)
    factors = [jnp.exp(one - top) for one in tops]
    total = functools.reduce(jnp.add, [f * one for f, one in zip(factors, sums)])
    shares = [
        pltpu.roll(f / total, lax.rem(2 * QH - me * heads, 2 * QH), 1) for f in factors
    ]
    mixed = []
    for h in range(heads):
        at = slice(h * row_count, (h + 1) * row_count)
        mixed.append(
            functools.reduce(
                jnp.add,
                [
                    message[at, :].astype(jnp.float32) * share[:, h : h + 1]
                    for share, message in zip(shares, messages)
                ],
            )
        )
    attention = jnp.concatenate(mixed, axis=1).astype(jnp.bfloat16)

    for at in range(0, coded.shape[1], PIECE):
        product[:, at : at + PIECE] = jnp.dot(
            attention, weight[:, at : at + PIECE], preferred_element_type=jnp.float32
        )
    turned = rotate(product[...], hadamard[...])
    coded[...] = jnp.clip(turned / quant_scale[...], -coded_most, coded_most).astype(
        jnp.bfloat16
    )


def finish_kernel(*refs):
    *terms, quant_scale, hadamard, residual, gain, new_residual, normed = refs
    summed = functools.reduce(jnp.add, [t[...].astype(jnp.float32) for t in terms])
    restored = rotate(summed * quant_scale[...], hadamard[...])
    combined = residual[...].astype(jnp.float32) + restored
    mean_square = jnp.mean(combined * combined, axis=1, keepdims=True)
    new_residual[...] = combined.astype(jnp.bfloat16)
    normed[...] = (
        combined * lax.rsqrt(mean_square + norm_eps) * gain[...].astype(jnp.float32)
    ).astype(jnp.bfloat16)


VM = pl.BlockSpec(memory_space=pltpu.VMEM)
SM = pl.BlockSpec(memory_space=pltpu.SMEM)
ANY = pl.BlockSpec(memory_space=pl.ANY)
MIB = 1 << 20


def in_hbm(array):
    return pltpu.with_memory_space_constraint(array, pltpu.HBM)


def body(
    queries,
    key_cache,
    value_cache,
    new_key,
    new_value,
    lengths,
    out_weight,
    quant_scale,
    residual,
    norm_gain,
):
    row_count, places, kv_width = key_cache.shape
    parts = lax.axis_size("tensor")
    width = out_weight.shape[1]
    chunk = QH // parts * row_count
    hadamard = jnp.asarray(hadamard_tile(), jnp.bfloat16)
    scale_row = quant_scale.reshape(1, width)
    gain_row = norm_gain.reshape(1, width)
    bf16 = jnp.bfloat16

    with jax.named_scope("attend"):
        messages = pl.pallas_call(
            functools.partial(attend_kernel, parts),
            out_shape=[
                jax.ShapeDtypeStruct((chunk + STATS, HD), bf16) for _ in range(parts)
            ],
            in_specs=[ANY] * 7,
            out_specs=[VM] * parts,
            scratch_shapes=[
                pltpu.SMEM(lengths.shape, jnp.int32),
                pltpu.VMEM(queries.shape, bf16),
                pltpu.VMEM(new_key.shape, bf16),
                pltpu.VMEM(new_value.shape, bf16),
                pltpu.VMEM((row_count, places + EXTRA, kv_width), bf16),
                pltpu.VMEM((row_count, places + EXTRA, kv_width), bf16),
                pltpu.VMEM((QH * row_count, HD), jnp.float32),
                pltpu.VMEM((QH * row_count, HD), jnp.float32),
                pltpu.SemaphoreType.DMA((4,)),
                pltpu.SemaphoreType.DMA((3,)),
            ],
            compiler_params=pltpu.CompilerParams(vmem_limit_bytes=12 * MIB),
        )(
            *[
                in_hbm(array)
                for array in (
                    lengths,
                    queries,
                    new_key,
                    new_value,
                    key_cache,
                    value_cache,
                    out_weight,
                )
            ],
        )

    def paired(array, s):
        return lax.ppermute(array, "tensor", [(i, i ^ s) for i in range(parts)])

    def shifted(array, s):
        return lax.ppermute(
            array, "tensor", [(i, (i + s) % parts) for i in range(parts)]
        )

    with jax.named_scope("exchange"):
        half = parts // 2
        order = [*range(half, parts), *range(1, half)]
        gathered = [messages[0]] + [paired(messages[s], s) for s in order]

    with jax.named_scope("project"):
        coded = pl.pallas_call(
            functools.partial(project_kernel, parts),
            out_shape=jax.ShapeDtypeStruct((row_count, width), bf16),
            in_specs=[VM] * (parts + 3),
            out_specs=VM,
            scratch_shapes=[
                pltpu.VMEM((row_count, width), jnp.float32),
            ],
            compiler_params=pltpu.CompilerParams(vmem_limit_bytes=16 * MIB),
        )(
            *gathered,
            pltpu.with_memory_space_constraint(out_weight, pltpu.VMEM),
            scale_row,
            hadamard,
        )

    with jax.named_scope("reduce"):
        order = [parts - 1, *range(1, parts - 1)]
        terms = [coded] + [shifted(coded, s) for s in order]

    with jax.named_scope("finish"):
        return pl.pallas_call(
            finish_kernel,
            out_shape=[jax.ShapeDtypeStruct((row_count, width), bf16)] * 2,
            in_specs=[VM] * (parts + 4),
            out_specs=[VM] * 2,
            compiler_params=pltpu.CompilerParams(vmem_limit_bytes=16 * MIB),
        )(*terms, scale_row, hadamard, residual, gain_row)


def solution(mesh):
    placed = (
        P(("groups", "dp"), None),
        P(("groups", "dp"), "tensor", None),
        P(("groups", "dp"), "tensor", None),
        P(("groups", "dp"), None),
        P(("groups", "dp"), None),
        P(("groups", "dp")),
        P("tensor", None),
        P(),
        P(("groups", "dp"), None),
        P(),
    )
    return jax.shard_map(
        body,
        mesh=mesh,
        in_specs=placed,
        out_specs=(P(("groups", "dp"), None), P(("groups", "dp"), None)),
        check_vma=False,
    )
```
